256 devices in a mesh: ctx: 32 (over x_lo, z, core), tp: 8 (over y, x_hi).
Axes of the slice: x: 4 (x_hi: 2, x_lo: 2; x = x_hi * 2 + x_lo), y: 4, z: 8, core: 2. Of those that a mesh axis runs over, the one named last changes fastest.
Arguments:
- query: bfloat16 [24576, 4096], P('ctx', 'tp'), may hold values from -36 to 36
- key: bfloat16 [24576, 1024], P('ctx', 'tp'), may hold values from -32 to 32
- value: bfloat16 [24576, 1024], P('ctx', 'tp'), may hold values from -6 to 6
- keep_rank: int32 [32, 768], P('ctx'), may hold values from 0 to 767, each once within a row
- kept_count: int32 [32], replicated, may hold values from 1 to 768, 12288 in all
- out_weight: bfloat16 [4096, 8192], P('tp'), may hold values from -0.09375 to 0.09375
Outputs:
- mixed: bfloat16 [12288, 8192], P('ctx', 'tp')
The draws below stay inside these ranges and needn't reach their ends.
Inputs may be any that keep to these rules, and one draw needn't show every extreme that they name: `keep_rank`: each row is a permutation of 0 to 767. `kept_count`: the counts sum to 12288; the largest is exactly 768.
All inputs are finite; a program needn't handle non-finite values.
Results may differ from the reference program's by a relative error of at most 0.019.
The reference program's roundings to bfloat16 on the way count: a program that leaves them out, or rounds other values in their place, can miss the bound.
Values may be sent and summed in bfloat16 or wider, within the bound.
A program may use at most 128 MiB of HBM per device.

```python
import math
import jax
import jax.numpy as jnp
import numpy as np
from jax import lax

D = 8192
HD = 128
KVH = 8
HQ = 32
ORIG_DEV = 768
KEPT = 12288
ORIG = 24576
N_CTX = 32
N_TP = 8


def draw_query(key, part):
    key = jax.random.fold_in(key, 1)
    return (3.0 * jnp.clip(jax.random.normal(key, (ORIG, HQ * HD), jnp.float32), -6.0, 6.0)).astype(jnp.bfloat16)


def draw_key(key, part):
    key = jax.random.fold_in(key, 2)
    return jnp.clip(jax.random.normal(key, (ORIG, KVH * HD), jnp.float32), -6.0, 6.0).astype(jnp.bfloat16)


def block_scale(stream_key, extent, shards, low, largest):
    factor_of, own = 1.0, jax.random.fold_in(stream_key, 6)
    for axis_at, shards_of in shards:
        draws = jnp.exp(jax.random.uniform(jax.random.fold_in(own, axis_at), (shards_of,), jnp.float32, low / len(shards), largest / len(shards)))
        factor_of = factor_of * jnp.repeat(draws, extent[axis_at] // shards_of).reshape([-1 if axis == axis_at else 1 for axis in range(len(extent))])
    return factor_of


def length_profile(count, total, bound, skew):
    portions = [(1 << 20) // math.isqrt(grade ** skew) + 1 for grade in range(2, count + 1)]
    surplus, counts = total - bound - (count - 1), [1] * (count - 1)
    while surplus > 0:
        movable = [i for i in range(count - 1) if counts[i] < bound]
        mass, budget = sum([portions[i] for i in movable]), surplus
        for i in movable:
            extra = min(bound - counts[i], max(1, budget * portions[i] // mass), surplus)
            counts[i] = counts[i] + extra
            surplus = surplus - extra
    return np.array([bound] + counts)


def uneven_parts(key, count, total, reach, lean):
    if count == 2:
        one = jax.random.randint(key, (), max(1, total - reach), min(reach, total - 1) + 1)
        return jnp.stack([one, total - one])
    sizes = jnp.asarray(length_profile(count, total, reach, lean), jnp.int32)
    couples = (count - 1) // 2
    giver, receiver = sizes[1:1 + 2 * couples:2], sizes[2:2 + 2 * couples:2]
    margin = jnp.minimum(giver - 1, reach - receiver)
    passed = jax.random.randint(jax.random.fold_in(key, 1), (couples,), 0, 1 << 20) % (margin + 1)
    sizes = sizes.at[1:1 + 2 * couples:2].set(giver - passed).at[2:2 + 2 * couples:2].set(receiver + passed)
    return sizes[jax.random.permutation(jax.random.fold_in(key, 2), count)]


def gaussian(key, shape, deviation, reach, shards=(), kind=jnp.bfloat16):
    gain = block_scale(key, shape, shards, -0.22, 0.18) if shards else 1.0
    drawn = jax.random.normal(key, shape, jnp.float32) * deviation * gain
    return jnp.minimum(jnp.maximum(drawn, -reach), reach).astype(kind)


def setup_inputs(seed: int = 0) -> dict:
    keys = jax.random.split(jax.random.key(seed), 7)
    return {
        "query": draw_query(jax.random.fold_in(keys[6], 71), 0),
        "key": draw_key(jax.random.fold_in(keys[6], 71), 0),
        "value": gaussian(keys[2], (ORIG, KVH * HD), 1.0, 6.0, ((0, 32), (1, 8))),
        "keep_rank": jax.vmap(lambda own: jax.random.permutation(own, ORIG_DEV))(jax.random.split(keys[3], N_CTX)).reshape((N_CTX, ORIG_DEV)).astype(jnp.int32),
        "kept_count": uneven_parts(keys[4], N_CTX, KEPT, ORIG_DEV, 2).astype(jnp.int32),
        "out_weight": gaussian(keys[5], (HQ * HD, D), (HQ * HD) ** -0.5, 0.09375, ((0, 8),)),
    }


rope_base = 1000000.0
masked_score = -1e+30

def rotate(rows, positions, heads):
    count_rows = rows.shape[0]
    half_dim = HD // 2
    as_float = rows.astype(jnp.float32).reshape(count_rows, heads, HD)
    inv_freq = rope_base ** (-(jnp.arange(half_dim, dtype=jnp.float32) * 2.0 / HD))
    angles = positions.astype(jnp.float32)[:, None] * inv_freq[None, :]
    cosine = jnp.cos(angles)[:, None, :]
    sine = jnp.sin(angles)[:, None, :]
    first_half = as_float[..., :half_dim]
    second_half = as_float[..., half_dim:]
    turned = jnp.concatenate([first_half * cosine - second_half * sine, second_half * cosine + first_half * sine], axis=-1)
    return turned.reshape(count_rows, heads * HD).astype(jnp.bfloat16)

def reference(query, key, value, keep_rank, kept_count, out_weight):
    kept_mask = (keep_rank < kept_count[:, None]).reshape(-1)
    chosen = jnp.nonzero(kept_mask, size=KEPT)[0].astype(jnp.int32)
    rot_query = rotate(query[chosen], chosen, HQ)
    rot_key = rotate(key[chosen], chosen, KVH)
    kept_value = value[chosen]
    group_size = HQ // KVH
    key_float = rot_key.astype(jnp.float32).reshape(KEPT, KVH, HD)
    value_float = kept_value.astype(jnp.float32).reshape(KEPT, KVH, HD)
    block_rows = 256
    query_blocks = rot_query.reshape(KEPT // block_rows, block_rows, KVH, group_size, HD)
    block_starts = jnp.arange(KEPT // block_rows, dtype=jnp.int32) * block_rows
    key_index = jnp.arange(KEPT, dtype=jnp.int32)

    def attend(pair):
        query_block, block_start = pair
        scores = jnp.einsum('bkgd,pkd->kgbp', query_block.astype(jnp.float32), key_float) / math.sqrt(HD)
        row_index = block_start + jnp.arange(block_rows, dtype=jnp.int32)
        allowed = key_index[None, :] <= row_index[:, None]
        scores = jnp.where(allowed, scores, masked_score)
        row_max = lax.optimization_barrier(jnp.max(scores, axis=-1, keepdims=True))
        weights = jnp.where(allowed, jnp.exp(scores - row_max), 0.0)
        row_total = lax.optimization_barrier(jnp.sum(weights, axis=-1))
        weights_b = weights.astype(jnp.bfloat16)
        summed = jnp.einsum('kgbp,pkd->bkgd', weights_b.astype(jnp.float32), value_float)
        result = summed / jnp.transpose(row_total, (2, 0, 1))[..., None]
        return result.reshape(block_rows, HQ * HD).astype(jnp.bfloat16)
    attention = lax.map(attend, (query_blocks, block_starts)).reshape(KEPT, HQ * HD)
    group_width = HQ * HD // N_TP
    attention_groups = jnp.transpose(attention.reshape(KEPT, N_TP, group_width), (1, 0, 2))
    weight_groups = out_weight.reshape(N_TP, group_width, D)

    def add_group(running, pair):
        attention_part, weight_part = pair
        partial_term = jnp.dot(attention_part, weight_part, preferred_element_type=jnp.float32).astype(jnp.bfloat16)
        partial_term = lax.optimization_barrier(partial_term)
        return (running + partial_term.astype(jnp.float32), None)
    summed_all, _ = lax.scan(add_group, jnp.zeros((KEPT, D), jnp.float32), (attention_groups, weight_groups))
    return summed_all.astype(jnp.bfloat16)
```

```python
import functools
import math

import jax
import jax.numpy as jnp
import numpy as np
from jax import lax
from jax.experimental import pallas as pl
from jax.experimental.pallas import tpu as pltpu
from jax.sharding import PartitionSpec as P

HD = 128
ROWS = 768
BLK = 48
CHIPS = 16
SHARDS = 32
KEPT = 12288
MESH = pl.DeviceIdType.MESH
VMEM = pltpu.VMEM
BF = jnp.bfloat16
F32 = jnp.float32


def tables():
    freq = 1000000.0 ** (-(np.arange(HD // 2) * 2.0 / HD))
    sign = np.concatenate([-np.ones(HD // 2), np.ones(HD // 2)])
    both = np.concatenate([freq, freq])
    own = np.arange(ROWS)[:, None] * both
    base = (np.arange(SHARDS) * ROWS)[:, None] * both
    col = np.arange(SHARDS * BLK)
    cols = np.zeros((8, SHARDS * BLK), np.int32)
    cols[0], cols[1] = col // BLK, col % BLK
    f = lambda a: a.astype(np.float32)
    return (f(np.cos(own)), f(np.sin(own) * sign), f(np.cos(base)), f(np.sin(base) * sign), cols)


def place():
    c, t = lax.axis_index("ctx"), lax.axis_index("tp")
    return dict(c=c, t=t, core=c % 2, z=(c // 2) % 8, xl=c // 16, j=c // 2, y=t // 2, xh=t % 2)


def ctx_of(xl, z, core):
    return xl * 16 + z * 2 + core


def remote(src, dst, ssem, rsem, dev):
    return pltpu.make_async_remote_copy(
        src_ref=src, dst_ref=dst, send_sem=ssem, recv_sem=rsem, device_id=dev, device_id_type=MESH)


def exchange_kernel(cnt, rank, q, k, v, ci, si, cb, sb, cols, w,
                    qo, kv, wf,
                    xs, sq, skv, rq, rkv, unp,
                    kv_s, kv_r, q_s, q_r, ring_s, ring_r, die_r, w_s, w_r, wd_s, wd_r, loc):
    me = place()
    c, t, core, z, xl, j, y, xh = (me[n] for n in ("c", "t", "core", "z", "xl", "j", "y", "xh"))
    bar = pltpu.get_barrier_semaphore()

    def hail(i, _):
        pl.semaphore_signal(bar, inc=1, device_id=((c + i) % SHARDS, t), device_id_type=MESH)
        return 0
    lax.fori_loop(1, SHARDS, hail, 0)
    cx = ctx_of(1 - xl, z, core)
    w_peers = [(c, ((y + d) % 4) * 2 + xh) for d in (1, 2, 3)]
    w_peers += [(cx, ((y + d) % 4) * 2 + (1 - xh)) for d in (0, 1, 2, 3)]
    for peer in w_peers:
        pl.semaphore_signal(bar, inc=1, device_id=peer, device_id_type=MESH)

    cbr, sbr = cb[pl.ds(c, 1), :], sb[pl.ds(c, 1), :]
    civ, siv = ci[...], si[...]
    cosv = civ * cbr - siv * sbr
    sinv = siv * cbr + civ * sbr
    scale = math.log2(math.e) / math.sqrt(HD)
    for h in range(5):
        src = k[...] if h == 4 else q[:, h * HD:(h + 1) * HD]
        x = src.astype(F32)
        out = x * cosv + pltpu.roll(x, HD // 2, 1) * sinv
        if h < 4:
            out = out * scale
        xs[:, h * HD:(h + 1) * HD] = out.astype(BF)
    xs[:, 5 * HD:] = v[...]

    my_count = cnt[c]
    start = jnp.int32(0)
    for s in range(SHARDS):
        start = start + jnp.where(s < c, cnt[s], 0)
    kept = rank[...] < my_count
    keptf = jnp.where(kept, 1.0, 0.0).astype(BF)
    i0 = lax.broadcasted_iota(jnp.int32, (ROWS, ROWS), 0)
    i1 = lax.broadcasted_iota(jnp.int32, (ROWS, ROWS), 1)
    tri = jnp.where(i0 < i1, 1.0, 0.0).astype(BF)
    order = jnp.dot(jnp.broadcast_to(keptf, (16, ROWS)), tri, preferred_element_type=F32)[0:1]
    slot = order.astype(jnp.int32) + lax.rem(start, jnp.int32(ROWS))
    slot = jnp.where(slot >= ROWS, slot - ROWS, slot)
    slot = jnp.where(kept, slot, -1)
    perm = jnp.where(i0 == slot, 1.0, 0.0).astype(BF)
    kvp = jnp.dot(perm, xs[:, 4 * HD:], preferred_element_type=F32).astype(BF)
    skv[0] = kvp[:, :HD]
    skv[1] = kvp[:, HD:]

    pl.semaphore_wait(bar, SHARDS - 1 + 7)

    def kv_copy(d):
        dj = d // 2
        return remote(skv.at[d % 2, pl.ds(pl.multiple_of(dj * BLK, BLK), BLK)],
                      rkv.at[pl.ds(pl.multiple_of(c * BLK, BLK), BLK)],
                      kv_s.at[d], kv_r.at[c], (d, t))

    def q_copy(d):
        dj = d // 2
        return remote(sq.at[d % 2, pl.ds(pl.multiple_of(dj * BLK, BLK), BLK)],
                      rq.at[pl.ds(pl.multiple_of(c * BLK, BLK), BLK)],
                      q_s.at[d], q_r.at[c], (d, t))

    def start_kv(i, _):
        kv_copy((c + i) % SHARDS).start()
        return 0
    lax.fori_loop(1, SHARDS, start_kv, 0)
    own_rows = pl.ds(pl.multiple_of(j * BLK, BLK), BLK)
    to_rows = pl.ds(pl.multiple_of(c * BLK, BLK), BLK)
    own_kv = pltpu.make_async_copy(skv.at[core, own_rows], rkv.at[to_rows], loc.at[0])
    own_kv.start()

    half = 256

    def w_copy(n):
        peer = w_peers[n]
        return remote(w.at[pl.ds(pl.multiple_of(core * half, half), half),
                           pl.ds(pl.multiple_of(peer[1] * 1024, 1024), 1024)],
                      wf.at[pl.ds(pl.multiple_of(t * 512 + core * half, half), half)],
                      w_s.at[n], w_r.at[t], peer)
    for n in range(7):
        w_copy(n).start()
    w_own = pltpu.make_async_copy(
        w.at[:, pl.ds(pl.multiple_of(t * 1024, 1024), 1024)],
        wf.at[pl.ds(pl.multiple_of(t * 512, 512), 512)], loc.at[2])
    w_own.start()

    qp = jnp.dot(perm, xs[:, :4 * HD], preferred_element_type=F32).astype(BF)
    sq[0] = qp[:, :2 * HD]
    sq[1] = qp[:, 2 * HD:]

    def start_q(i, _):
        q_copy((c + i) % SHARDS).start()
        return 0
    lax.fori_loop(1, SHARDS, start_q, 0)
    own_q = pltpu.make_async_copy(sq.at[core, own_rows], rq.at[to_rows], loc.at[1])
    own_q.start()

    grp, mod = cols[0:1, :], cols[1:2, :]
    first = jnp.zeros((1, SHARDS * BLK), jnp.int32)
    last = jnp.zeros((1, SHARDS * BLK), jnp.int32)
    for s in range(SHARDS):
        first = first + jnp.where(grp > s, cnt[s], 0)
        last = last + jnp.where(grp >= s, cnt[s], 0)
    isub = lax.broadcasted_iota(jnp.int32, (BLK, SHARDS * BLK), 0)
    for lv in range(CHIPS):
        num = mod + (lv * ROWS + j * BLK)
        sel = jnp.where((first <= num) & (num < last), mod, -1)
        unp[lv * BLK:(lv + 1) * BLK, :] = jnp.where(isub == sel, 1.0, 0.0).astype(BF)

    own_kv.wait()

    def wait_kv(i, _):
        d = (c + SHARDS - i) % SHARDS
        remote(skv.at[0, pl.ds(0, BLK)], rkv.at[pl.ds(pl.multiple_of(d * BLK, BLK), BLK)],
               kv_s.at[d], kv_r.at[d], (d, t)).wait_recv()
        return 0
    lax.fori_loop(1, SHARDS, wait_kv, 0)
    mine = jnp.dot(unp[...], rkv[...], preferred_element_type=F32).astype(BF)
    for lv in range(CHIPS):
        kv[core, lv, j] = mine[lv * BLK:(lv + 1) * BLK]

    def block(b):
        return kv.at[core, :, b]

    def ring(b, way):
        dev = [(ctx_of(xl, (z + 1) % 8, core), t), (ctx_of(xl, (z + 7) % 8, core), t),
               (ctx_of(1 - xl, z, core), t), (c + 1 - 2 * core, t)][way]
        rsem = die_r.at[b] if way == 3 else ring_r.at[b]
        return remote(block(b), block(b), ring_s.at[way, b], rsem, dev)
    started = []

    def go(b, way):
        cp = ring(b, way)
        cp.start()
        started.append(cp)

    def arrive(b):
        remote(block(b), block(b), ring_s.at[0, b], ring_r.at[b], (c, t)).wait_recv()

    for way in (2, 0, 1, 3):
        go(j, way)
    jx = (1 - xl) * 8 + z
    arrive(jx)
    for way in (0, 1, 3):
        go(jx, way)
    for d in range(1, 5):
        zl, zr = (z + 8 - d) % 8, (z + d) % 8
        for col, rmax, lmax in ((xl, 4, 3), (1 - xl, 3, 4)):
            if d <= rmax:
                b = col * 8 + zl
                arrive(b)
                if d < rmax:
                    go(b, 0)
                go(b, 3)
            if d <= lmax:
                b = col * 8 + zr
                arrive(b)
                if d < lmax:
                    go(b, 1)
                go(b, 3)
        if d == 1:
            own_q.wait()

            def wait_q(i, _):
                e = (c + SHARDS - i) % SHARDS
                remote(sq.at[0, pl.ds(0, BLK)], rq.at[pl.ds(pl.multiple_of(e * BLK, BLK), BLK)],
                       q_s.at[e], q_r.at[e], (e, t)).wait_recv()
                return 0
            lax.fori_loop(1, SHARDS, wait_q, 0)
            qo[...] = jnp.dot(unp[...], rq[...], preferred_element_type=F32).astype(BF)

    w_own.wait()

    def half_rows(b, cr):
        return wf.at[pl.ds(pl.multiple_of(b * 512 + cr * half, half), half)]
    passed = []
    for n in range(7):
        b = w_peers[n][1]
        remote(half_rows(b, core), half_rows(b, core), w_s.at[n], w_r.at[b], (c, t)).wait_recv()
        cp = remote(half_rows(b, core), half_rows(b, core), wd_s.at[n], wd_r.at[b],
                    (c + 1 - 2 * core, t))
        cp.start()
        passed.append(cp)
    for n in range(7):
        b = w_peers[n][1]
        remote(half_rows(b, core), half_rows(b, 1 - core), wd_s.at[n], wd_r.at[b],
               (c, t)).wait_recv()
    for cp in passed:
        cp.wait_send()
    for n in range(7):
        w_copy(n).wait_send()
    for cp in started:
        cp.wait_send()

    def wait_die(b, _):
        ref = kv.at[1 - core, :, b]
        remote(ref, ref, ring_s.at[3, b], die_r.at[b], (c, t)).wait_recv()
        return 0
    lax.fori_loop(0, CHIPS, wait_die, 0)

    def wait_sends(i, _):
        d = (c + i) % SHARDS
        kv_copy(d).wait_send()
        q_copy(d).wait_send()
        return 0
    lax.fori_loop(1, SHARDS, wait_sends, 0)


def exchange(cnt, rank, q, k, v, w):
    dma = pltpu.SemaphoreType.DMA
    consts = [jnp.asarray(a) for a in tables()]
    vm = pl.BlockSpec(memory_space=VMEM)
    return pl.pallas_call(
        exchange_kernel,
        out_shape=[jax.ShapeDtypeStruct((ROWS, 2 * HD), BF),
                   jax.ShapeDtypeStruct((2, CHIPS, CHIPS, BLK, HD), BF),
                   jax.ShapeDtypeStruct((4096, 1024), BF)],
        in_specs=[pl.BlockSpec(memory_space=pltpu.SMEM)] + [vm] * 9 + [pl.BlockSpec(memory_space=pl.ANY)],
        out_specs=[vm, vm, pl.BlockSpec(memory_space=pl.ANY)],
        scratch_shapes=[
            VMEM((ROWS, 6 * HD), BF), VMEM((2, ROWS, 2 * HD), BF), VMEM((2, ROWS, HD), BF),
            VMEM((SHARDS * BLK, 2 * HD), BF), VMEM((SHARDS * BLK, HD), BF), VMEM((ROWS, SHARDS * BLK), BF),
            dma((SHARDS,)), dma((SHARDS,)), dma((SHARDS,)), dma((SHARDS,)),
            dma((4, CHIPS)), dma((CHIPS,)), dma((CHIPS,)),
            dma((8,)), dma((8,)), dma((8,)), dma((8,)), dma((3,)),
        ],
        compiler_params=pltpu.CompilerParams(
            collective_id=0, has_side_effects=True, vmem_limit_bytes=48 << 20),
        name="exchange",
    )(cnt, rank, q, k, v, *consts, w)


QL = 4
KC = 768


def attend_kernel(q, kv, o, qs):
    j = lax.axis_index("ctx") // 2
    tok = QL * BLK
    rows = 2 * tok
    for b in range(CHIPS // QL):
        qs[:tok] = q[b * tok:(b + 1) * tok, :HD]
        qs[tok:] = q[b * tok:(b + 1) * tok, HD:]
        qv = qs[...]

        def step(kc, state, masked):
            m, l, acc = state
            at = pl.ds(pl.multiple_of(kc * KC, KC), KC)
            s = lax.dot_general(qv, kv[0, at, :], (((1,), (1,)), ((), ())), preferred_element_type=F32)
            if masked is not None:
                r = lax.broadcasted_iota(jnp.int32, (rows, KC), 0)
                r = jnp.where(r >= tok, r - tok, r)
                lim = jnp.full((rows, KC), -1, jnp.int32)
                lim = jnp.where(r >= (masked + 1) * BLK, KC, lim)
                inside = (r >= masked * BLK) & (r < (masked + 1) * BLK)
                lim = jnp.where(inside, r - masked * BLK + j * BLK, lim)
                col = lax.broadcasted_iota(jnp.int32, (rows, KC), 1)
                s = jnp.where(col <= lim, s, -1e30)
            mn = jnp.maximum(m, jnp.max(s, axis=1, keepdims=True))
            a = jnp.exp2(m - mn)
            p = jnp.exp2(s - mn)
            l = l * a + jnp.sum(p, axis=1, keepdims=True)
            acc = acc * a + jnp.dot(p.astype(BF), kv[1, at, :], preferred_element_type=F32)
            return mn, l, acc

        state = (jnp.full((rows, 1), -1e30, F32), jnp.zeros((rows, 1), F32), jnp.zeros((rows, HD), F32))
        if b > 0:
            state = lax.fori_loop(0, b * QL, lambda kc, st: step(kc, st, None), state)
        for lv in range(QL):
            state = step(b * QL + lv, state, lv)
        m, l, acc = state
        out = (acc / l).astype(BF)
        o[b * tok:(b + 1) * tok, :HD] = out[:tok]
        o[b * tok:(b + 1) * tok, HD:] = out[tok:]


def attend(q, kv):
    vm = pl.BlockSpec(memory_space=VMEM)
    return pl.pallas_call(
        attend_kernel,
        out_shape=jax.ShapeDtypeStruct((ROWS, 2 * HD), BF),
        in_specs=[vm, vm],
        out_specs=vm,
        scratch_shapes=[VMEM((2 * QL * BLK, HD), BF)],
        compiler_params=pltpu.CompilerParams(vmem_limit_bytes=48 << 20),
        name="attend",
    )(q, kv)


def project_kernel(att, w, out, af, wv, acc, a_s, a_r, g_s, g_r, loc):
    me = place()
    c, t, core, z, xl, j, y, xh = (me[n] for n in ("c", "t", "core", "z", "xl", "j", "y", "xh"))
    bar = pltpu.get_barrier_semaphore()
    load = pltpu.make_async_copy(w, wv, loc.at[0])
    load.start()

    def target(lv):
        return 2 * lv + xl

    def source(n):
        return ctx_of(core, n // 2, n % 2)

    for lv in range(CHIPS):
        pl.semaphore_signal(bar, inc=1, device_id=(target(lv), t), device_id_type=MESH)
    for n in range(CHIPS):
        pl.semaphore_signal(bar, inc=1, device_id=(source(n), t), device_id_type=MESH)
    gat = [(c, y * 2 + 1 - xh), (c, ((y + 1) % 4) * 2 + xh), (c, ((y + 3) % 4) * 2 + xh)]
    for dev in gat:
        pl.semaphore_signal(bar, inc=1, device_id=dev, device_id_type=MESH)
    pl.semaphore_wait(bar, 2 * CHIPS + 3)

    slot = z * 2 + core
    here = (pl.ds(pl.multiple_of((j % 8) * BLK, BLK), BLK), pl.ds(pl.multiple_of(core * 256, 256), 256))

    def place_copy(lv):
        return remote(att.at[pl.ds(lv * BLK, BLK)], af.at[(t,) + here], a_s.at[lv], a_r.at[slot],
                      (target(lv), t))

    def own_copy(lv):
        return pltpu.make_async_copy(att.at[pl.ds(lv * BLK, BLK)], af.at[(t,) + here], loc.at[1])

    for lv in range(CHIPS):
        @pl.when(target(lv) != c)
        def _():
            place_copy(lv).start()

        @pl.when(target(lv) == c)
        def _():
            own_copy(lv).start()
    for n in range(CHIPS):
        rows = pl.ds((n // 2) * BLK, BLK)
        cs = pl.ds((n % 2) * 256, 256)

        @pl.when(source(n) != c)
        def _():
            remote(att.at[pl.ds(0, BLK)], af.at[t, rows, cs], a_s.at[n], a_r.at[n], (c, t)).wait_recv()

        @pl.when(source(n) == c)
        def _():
            own_copy(0).wait()

    sent = []

    def go(b, way):
        cp = remote(af.at[b], af.at[b], g_s.at[way, b], g_r.at[b], gat[way])
        cp.start()
        sent.append(cp)

    def arrive(b):
        remote(af.at[b], af.at[b], g_s.at[0, b], g_r.at[b], (c, t)).wait_recv()

    def mul(b, first=False):
        rows = pl.ds(pl.multiple_of(b * 512, 512), 512)

        @pl.loop(0, 4)
        def _(n):
            cs = pl.ds(pl.multiple_of(n * 256, 256), 256)
            part = jnp.dot(af[b], wv[rows, cs], preferred_element_type=F32)
            acc[:, cs] = part if first else acc[:, cs] + part

    for way in (0, 1, 2):
        go(t, way)
    load.wait()
    mul(t, True)
    bx = y * 2 + 1 - xh
    arrive(bx)
    go(bx, 1)
    go(bx, 2)
    mul(bx)
    lo, hi, opp = (y + 3) % 4, (y + 1) % 4, (y + 2) % 4
    arrive(lo * 2 + xh)
    go(lo * 2 + xh, 1)
    mul(lo * 2 + xh)
    arrive(hi * 2 + xh)
    mul(hi * 2 + xh)
    arrive(hi * 2 + 1 - xh)
    go(hi * 2 + 1 - xh, 2)
    mul(hi * 2 + 1 - xh)
    arrive(lo * 2 + 1 - xh)
    mul(lo * 2 + 1 - xh)
    arrive(opp * 2 + xh)
    mul(opp * 2 + xh)
    arrive(opp * 2 + 1 - xh)
    mul(opp * 2 + 1 - xh)
    out[...] = acc[...].astype(BF)
    for cp in sent:
        cp.wait_send()
    for lv in range(CHIPS):
        @pl.when(target(lv) != c)
        def _():
            place_copy(lv).wait_send()


def project(att, w):
    dma = pltpu.SemaphoreType.DMA
    vm = pl.BlockSpec(memory_space=VMEM)
    return pl.pallas_call(
        project_kernel,
        out_shape=jax.ShapeDtypeStruct((384, 1024), BF),
        in_specs=[vm, pl.BlockSpec(memory_space=pl.ANY)],
        out_specs=vm,
        scratch_shapes=[
            VMEM((8, 384, 512), BF), VMEM((4096, 1024), BF), VMEM((384, 1024), F32),
            dma((CHIPS,)), dma((CHIPS,)), dma((3, 8)), dma((8,)), dma((2,)),
        ],
        compiler_params=pltpu.CompilerParams(
            collective_id=1, has_side_effects=True, vmem_limit_bytes=48 << 20),
        name="project",
    )(att, w)


def local(query, key, value, keep_rank, kept_count, out_weight):
    q, kv, w = exchange(kept_count, keep_rank, query, key, value, out_weight)
    att = attend(q, kv.reshape(2, KEPT, HD))
    return project(att, w)


def solution(mesh):
    placed = (P("ctx", "tp"), P("ctx", "tp"), P("ctx", "tp"), P("ctx", None), P(), P("tp", None))
    return jax.shard_map(
        local, mesh=mesh, in_specs=placed, out_specs=P("ctx", "tp"), check_vma=False)
```

```python
import math

import jax
import jax.numpy as jnp
import numpy as np
from jax import lax
from jax.experimental import pallas as pl
from jax.experimental.pallas import tpu as pltpu
from jax.sharding import PartitionSpec as P

HD = 128
ROWS = 768
BLK = 48
CHIPS = 16
SHARDS = 32
SLOTS = SHARDS * BLK
QL = 4
GROUPS = CHIPS // QL
LROWS = 2 * BLK
QROWS = QL * LROWS
KC = 3072
OUT = 1024
NT = (((1,), (1,)), ((), ()))
MESH = pl.DeviceIdType.MESH
VMEM = pltpu.VMEM
BF = jnp.bfloat16
F32 = jnp.float32


def tables():
    freq = 1000000.0 ** (-(np.arange(HD // 2) * 2.0 / HD))
    sign = np.concatenate([-np.ones(HD // 2), np.ones(HD // 2)])
    both = np.concatenate([freq, freq])
    own = np.arange(ROWS)[:, None] * both
    base = (np.arange(SHARDS) * ROWS)[:, None] * both
    col = np.arange(SLOTS)
    cols = np.zeros((8, SLOTS), np.int32)
    cols[0], cols[1] = col // BLK, col % BLK
    f = lambda a, b: np.stack([np.cos(a), np.sin(b) * sign]).astype(np.float32)
    return f(own, own), f(base, base), cols


def ctx_of(xl, z, core):
    return xl * 16 + z * 2 + core


def remote(src, dst, ssem, rsem, dev):
    return pltpu.make_async_remote_copy(
        src_ref=src, dst_ref=dst, send_sem=ssem, recv_sem=rsem, device_id=dev, device_id_type=MESH)


def at16(first, size):
    return pl.ds(pl.multiple_of(first, 16), size)


def layer_kernel(cnt, rank_h, q_h, k_h, v_h, own_h, base_h, cols_h, w_h, out,
                 rank, qin, kin, vin, own, base, cols,
                 xs, sq, skv, rq, rkv, unp, qs, kv, m_s, acc_s, o_s, af, wf, po,
                 ld, kv_s, kv_r, q_s, q_r, ring_s, ring_r, die_r, w_s, w_r, wd_s, wd_r,
                 a_s, a_r, g_s, g_r):
    c, t = lax.axis_index("ctx"), lax.axis_index("tp")
    core, z, xl, j, y, xh = c % 2, (c // 2) % 8, c // 16, c // 2, t // 2, t % 2
    mate = c + 1 - 2 * core
    bar = pltpu.get_barrier_semaphore()

    loads = {}
    wcol = pl.ds(pl.multiple_of(t * OUT, OUT), OUT)
    for n, (name, src, dst) in enumerate([
            ("rank", rank_h, rank), ("k", k_h, kin), ("own", own_h, own), ("base", base_h, base),
            ("v", v_h, vin), ("q", q_h, qin), ("cols", cols_h, cols),
            ("w", w_h.at[:, wcol], wf.at[pl.ds(pl.multiple_of(t * 512, 512), 512)])]):
        loads[name] = pltpu.make_async_copy(src, dst, ld.at[n])
        loads[name].start()

    def hail(i, _):
        pl.semaphore_signal(bar, inc=1, device_id=((c + i) % SHARDS, t), device_id_type=MESH)
        return 0
    lax.fori_loop(1, SHARDS, hail, 0)
    cx = ctx_of(1 - xl, z, core)
    w_peers = [(c, ((y + d) % 4) * 2 + xh) for d in (1, 2, 3)]
    w_peers += [(cx, ((y + d) % 4) * 2 + (1 - xh)) for d in (0, 1, 2, 3)]
    gat = [(c, y * 2 + 1 - xh), (c, ((y + 1) % 4) * 2 + xh), (c, ((y + 3) % 4) * 2 + xh)]
    for peer in w_peers + gat[:1]:
        pl.semaphore_signal(bar, inc=1, device_id=peer, device_id_type=MESH)

    loads["rank"].wait()
    my_count = cnt[c]
    start = jnp.int32(0)
    for s in range(SHARDS):
        start = start + jnp.where(s < c, cnt[s], 0)
    kept = rank[...] < my_count
    keptf = jnp.where(kept, 1.0, 0.0).astype(BF)
    i0 = lax.broadcasted_iota(jnp.int32, (ROWS, ROWS), 0)
    i1 = lax.broadcasted_iota(jnp.int32, (ROWS, ROWS), 1)
    tri = jnp.where(i0 < i1, 1.0, 0.0).astype(BF)
    order = jnp.dot(jnp.broadcast_to(keptf, (16, ROWS)), tri, preferred_element_type=F32)[0:1]
    slot = order.astype(jnp.int32) + lax.rem(start, jnp.int32(ROWS))
    slot = jnp.where(slot >= ROWS, slot - ROWS, slot)
    slot = jnp.where(kept, slot, -1)
    perm = jnp.where(i0 == slot, 1.0, 0.0).astype(BF)

    for name in ("own", "base", "k", "v"):
        loads[name].wait()
    cbr, sbr = base[0, pl.ds(c, 1), :], base[1, pl.ds(c, 1), :]
    civ, siv = own[0], own[1]
    cosv = civ * cbr - siv * sbr
    sinv = siv * cbr + civ * sbr

    def rotate(x, scale):
        x = x.astype(F32)
        r = x * cosv + pltpu.roll(x, HD // 2, 1) * sinv
        return (r * scale if scale else r).astype(BF)
    xs[:, 4 * HD:5 * HD] = rotate(kin[...], None)
    xs[:, 5 * HD:] = vin[...]
    kvp = jnp.dot(perm, xs[:, 4 * HD:], preferred_element_type=F32).astype(BF)
    skv[0] = kvp[:, :HD]
    skv[1] = kvp[:, HD:]
    pl.semaphore_wait(bar, SHARDS - 1 + 8)

    def kv_copy(d):
        return remote(skv.at[d % 2, at16((d // 2) * BLK, BLK)], rkv.at[at16(c * BLK, BLK)],
                      kv_s.at[d], kv_r.at[c], (d, t))

    def q_copy(d):
        return remote(sq.at[d % 2, at16((d // 2) * BLK, BLK)], rq.at[at16(c * BLK, BLK)],
                      q_s.at[d], q_r.at[c], (d, t))

    def start_kv(i, _):
        kv_copy((c + i) % SHARDS).start()
        return 0
    lax.fori_loop(1, SHARDS, start_kv, 0)
    own_kv = pltpu.make_async_copy(skv.at[core, at16(j * BLK, BLK)], rkv.at[at16(c * BLK, BLK)], ld.at[8])
    own_kv.start()

    half = 256

    def half_rows(b, cr):
        return wf.at[pl.ds(pl.multiple_of(b * 512 + cr * half, half), half)]

    def w_copy(n):
        peer = w_peers[n]
        return remote(w_h.at[pl.ds(pl.multiple_of(core * half, half), half),
                             pl.ds(pl.multiple_of(peer[1] * OUT, OUT), OUT)],
                      half_rows(t, core), w_s.at[n], w_r.at[t], peer)
    for n in range(7):
        w_copy(n).start()

    scale = math.log2(math.e) / math.sqrt(HD)
    loads["q"].wait()
    for h in range(4):
        xs[:, h * HD:(h + 1) * HD] = rotate(qin[:, h * HD:(h + 1) * HD], scale)
    qp = jnp.dot(perm, xs[:, :4 * HD], preferred_element_type=F32).astype(BF)
    sq[0] = qp[:, :2 * HD]
    sq[1] = qp[:, 2 * HD:]

    def start_q(i, _):
        q_copy((c + i) % SHARDS).start()
        return 0
    lax.fori_loop(1, SHARDS, start_q, 0)
    own_q = pltpu.make_async_copy(sq.at[core, at16(j * BLK, BLK)], rq.at[at16(c * BLK, BLK)], ld.at[9])
    own_q.start()

    loads["cols"].wait()
    grp, mod = cols[0:1, :], cols[1:2, :]
    first = jnp.zeros((1, SLOTS), jnp.int32)
    last = jnp.zeros((1, SLOTS), jnp.int32)
    for s in range(SHARDS):
        first = first + jnp.where(grp > s, cnt[s], 0)
        last = last + jnp.where(grp >= s, cnt[s], 0)
    isub = lax.broadcasted_iota(jnp.int32, (BLK, SLOTS), 0)
    for lv in range(CHIPS):
        num = mod + (lv * ROWS + j * BLK)
        sel = jnp.where((first <= num) & (num < last), mod, -1)
        unp[lv * BLK:(lv + 1) * BLK, :] = jnp.where(isub == sel, 1.0, 0.0).astype(BF)
    m_s[...] = jnp.full(m_s.shape, -1e30, F32)
    acc_s[...] = jnp.zeros(acc_s.shape, F32)

    own_kv.wait()

    def wait_kv(i, _):
        d = (c + SHARDS - i) % SHARDS
        remote(skv.at[0, pl.ds(0, BLK)], rkv.at[at16(d * BLK, BLK)], kv_s.at[d], kv_r.at[d],
               (d, t)).wait_recv()
        return 0
    lax.fori_loop(1, SHARDS, wait_kv, 0)
    mine = jnp.dot(unp[...], rkv[...], preferred_element_type=F32).astype(BF)
    for lv in range(CHIPS):
        kv[core, lv, j] = mine[lv * BLK:(lv + 1) * BLK]

    sent = []
    ways = [(ctx_of(xl, (z + 1) % 8, core), t), (ctx_of(xl, (z + 7) % 8, core), t), (cx, t), (mate, t)]
    RIGHT, LEFT, CROSS, DIE = range(4)

    def piece(g, b):
        return kv.at[core, pl.ds(g * QL, QL), b]

    def go(g, b, *to):
        for way in to:
            rsem = die_r.at[g, b] if way == DIE else ring_r.at[g, b]
            cp = remote(piece(g, b), piece(g, b), ring_s.at[way, g, b], rsem, ways[way])
            cp.start()
            sent.append(cp)

    def arrive(g, b, *to):
        remote(piece(g, b), piece(g, b), ring_s.at[0, g, b], ring_r.at[g, b], (mate, t)).wait_recv()
        go(g, b, *to)

    def same(d):
        return xl * 8 + (z + 8 + d) % 8

    def other(d):
        return (1 - xl) * 8 + (z + 8 + d) % 8

    def tick(g, k):
        if k == 0:
            go(g, j, RIGHT, LEFT, CROSS, DIE)
        elif k == 1:
            arrive(g, other(0), RIGHT, LEFT, DIE)
            arrive(g, same(-1), RIGHT, DIE)
            arrive(g, same(1), LEFT, DIE)
        elif k == 2:
            arrive(g, other(-1), RIGHT, DIE)
            arrive(g, other(1), DIE)
            arrive(g, same(-2), RIGHT, DIE)
            arrive(g, same(2), LEFT, CROSS, DIE)
        elif k == 3:
            arrive(g, other(-2), DIE)
            arrive(g, same(-3), CROSS, DIE)
            arrive(g, same(3), LEFT, CROSS, DIE)
            arrive(g, other(2), DIE)
        else:
            arrive(g, same(4), CROSS, DIE)
            arrive(g, other(-3), DIE)
            arrive(g, other(3), DIE)
            arrive(g, other(4), DIE)

    def whole(g):
        def wait_die(b, _):
            ref = kv.at[1 - core, pl.ds(g * QL, QL), b]
            remote(ref, ref, ring_s.at[0, g, b], die_r.at[g, b], (mate, t)).wait_recv()
            return 0
        lax.fori_loop(0, CHIPS, wait_die, 0)

    def update(r0, n, s, vals):
        rows = pl.ds(r0, n)
        mo = m_s[rows, :]
        mn = jnp.maximum(mo, jnp.max(s, axis=1, keepdims=True))
        a = jnp.exp2(mo - mn)
        p = jnp.exp2(s - jnp.tile(mn, (1, s.shape[1] // HD))).astype(BF)
        m_s[rows, :] = mn
        vo = jnp.concatenate([vals, jnp.ones(vals.shape, BF)], axis=1)
        acc_s[rows, :] = acc_s[rows, :] * jnp.tile(a, (1, 2)) + jnp.dot(p, vo, preferred_element_type=F32)

    def unit(g, b):
        r0 = b * QROWS
        if b > g:
            n = QROWS // 2

            @pl.loop(0, QL * ROWS // KC)
            def _(i):
                lv = pl.ds(g * QL + i * (KC // ROWS), KC // ROWS)
                kk = kv[0, lv].reshape(KC, HD)
                vv = kv[1, lv].reshape(KC, HD)
                ss = [lax.dot_general(qs[r0 + h * n:r0 + (h + 1) * n, :], kk, NT, preferred_element_type=F32)
                      for h in range(2)]
                for h in range(2):
                    update(r0 + h * n, n, ss[h], vv)
            return
        for i in range(QL):
            lv = g * QL + i
            rs, n = r0 + i * LROWS, QROWS - i * LROWS
            kk = kv[0, lv].reshape(ROWS, HD)
            vv = kv[1, lv].reshape(ROWS, HD)
            s = lax.dot_general(qs[rs:rs + n, :], kk, NT, preferred_element_type=F32)
            r = lax.broadcasted_iota(jnp.int32, (LROWS, ROWS), 0)
            lim = jnp.where(r >= BLK, r - BLK, r) + j * BLK
            col = lax.broadcasted_iota(jnp.int32, (LROWS, ROWS), 1)
            top = jnp.where(col <= lim, s[:LROWS], -1e30)
            s = top if n == LROWS else jnp.concatenate([top, s[LROWS:]], axis=0)
            update(rs, n, s, vv)

    slot_a = z * 2 + core

    def here(h):
        return af.at[t, at16(z * BLK, BLK), pl.ds(pl.multiple_of(core * 256 + h * HD, HD), HD)]

    def o_copy(lv, h):
        return remote(o_s.at[pl.ds(lv * LROWS + h * BLK, BLK)], here(h), a_s.at[lv, h], a_r.at[slot_a, h],
                      (2 * lv + xl, t))

    def o_own(lv, h):
        return pltpu.make_async_copy(o_s.at[pl.ds(lv * LROWS + h * BLK, BLK)], here(h), ld.at[10 + h])

    def finish(b):
        rows = pl.ds(b * QROWS, QROWS)
        o_s[rows, :] = (acc_s[rows, :HD] / acc_s[rows, HD:]).astype(BF)
        for lv in range(b * QL, (b + 1) * QL):
            @pl.when(2 * lv + xl != c)
            def _():
                o_copy(lv, 0).start()
                o_copy(lv, 1).start()

            @pl.when(2 * lv + xl == c)
            def _():
                o_own(lv, 0).start()
                o_own(lv, 1).start()

    def take_queries():
        own_q.wait()

        def wait_q(i, _):
            e = (c + SHARDS - i) % SHARDS
            remote(sq.at[0, pl.ds(0, BLK)], rq.at[at16(e * BLK, BLK)], q_s.at[e], q_r.at[e],
                   (e, t)).wait_recv()
            return 0
        lax.fori_loop(1, SHARDS, wait_q, 0)
        r = jnp.dot(unp[...], rq[...], preferred_element_type=F32).astype(BF)
        for lv in range(CHIPS):
            for h in range(2):
                qs[lv * LROWS + h * BLK:lv * LROWS + (h + 1) * BLK, :] = r[
                    lv * BLK:(lv + 1) * BLK, h * HD:(h + 1) * HD]

    work = {g: [(g, b) for b in range(g, GROUPS)] for g in range(GROUPS)}
    ready, todo = 0, []
    for step in range(3 * (GROUPS - 1) + 5):
        for g in range(GROUPS):
            if 0 <= step - 3 * g <= 4:
                tick(g, step - 3 * g)
        if step == 4:
            take_queries()
        if step - 3 * ready == 4:
            whole(ready)
            todo += work[ready]
            ready += 1
        for _ in range(1 if ready < GROUPS else len(todo)):
            if todo:
                g, b = todo.pop(0)
                unit(g, b)
                if g == b:
                    finish(b)

    passed = []
    for n in range(7):
        b = w_peers[n][1]
        remote(half_rows(b, core), half_rows(b, core), w_s.at[n], w_r.at[b], (mate, t)).wait_recv()
        cp = remote(half_rows(b, core), half_rows(b, core), wd_s.at[n], wd_r.at[b], (mate, t))
        cp.start()
        passed.append(cp)
    loads["w"].wait()

    for n in range(CHIPS):
        src = ctx_of(core, n // 2, n % 2)
        for h in range(2):
            ref = af.at[t, pl.ds((n // 2) * BLK, BLK), pl.ds((n % 2) * 256 + h * HD, HD)]

            @pl.when(src != c)
            def _():
                remote(o_s.at[pl.ds(0, BLK)], ref, a_s.at[n, h], a_r.at[n, h], (mate, t)).wait_recv()

            @pl.when(src == c)
            def _():
                o_own(0, h).wait()

    def pass_on(b, *to):
        for way in to:
            cp = remote(af.at[b], af.at[b], g_s.at[way, b], g_r.at[b], gat[way])
            cp.start()
            sent.append(cp)

    def got(b, *to):
        remote(af.at[b], af.at[b], g_s.at[0, b], g_r.at[b], (mate, t)).wait_recv()
        pass_on(b, *to)

    def mul(b, begin=False):
        rows = pl.ds(pl.multiple_of(b * 512, 512), 512)
        if not begin:
            ref = half_rows(b, 1 - core)
            remote(ref, ref, wd_s.at[0], wd_r.at[b], (mate, t)).wait_recv()

        @pl.loop(0, OUT // 256)
        def _(n):
            cs = pl.ds(pl.multiple_of(n * 256, 256), 256)
            part = jnp.dot(af[b], wf[rows, cs], preferred_element_type=F32)
            po[:, cs] = part if begin else po[:, cs] + part

    lo, hi, opp = (y + 3) % 4, (y + 1) % 4, (y + 2) % 4
    pass_on(t, 0, 1, 2)
    mul(t, True)
    bx = y * 2 + 1 - xh
    got(bx, 1, 2)
    got(lo * 2 + xh, 1)
    mul(bx)
    mul(lo * 2 + xh)
    got(hi * 2 + xh)
    mul(hi * 2 + xh)
    got(hi * 2 + 1 - xh, 2)
    mul(hi * 2 + 1 - xh)
    got(lo * 2 + 1 - xh)
    mul(lo * 2 + 1 - xh)
    got(opp * 2 + xh)
    mul(opp * 2 + xh)
    got(opp * 2 + 1 - xh)
    mul(opp * 2 + 1 - xh)
    out[...] = po[...].astype(BF)

    for cp in passed + sent:
        cp.wait_send()
    for n in range(7):
        w_copy(n).wait_send()
    for lv in range(CHIPS):
        @pl.when(2 * lv + xl != c)
        def _():
            o_copy(lv, 0).wait_send()
            o_copy(lv, 1).wait_send()

    def wait_sends(i, _):
        d = (c + i) % SHARDS
        kv_copy(d).wait_send()
        q_copy(d).wait_send()
        return 0
    lax.fori_loop(1, SHARDS, wait_sends, 0)


def local(query, key, value, keep_rank, kept_count, out_weight):
    dma = pltpu.SemaphoreType.DMA
    consts = [jnp.asarray(a) for a in tables()]
    hbm = pl.BlockSpec(memory_space=pl.ANY)
    return pl.pallas_call(
        layer_kernel,
        out_shape=jax.ShapeDtypeStruct((384, OUT), BF),
        in_specs=[pl.BlockSpec(memory_space=pltpu.SMEM)] + [hbm] * 8,
        out_specs=pl.BlockSpec(memory_space=VMEM),
        scratch_shapes=[
            VMEM((1, ROWS), jnp.int32), VMEM((ROWS, 4 * HD), BF), VMEM((ROWS, HD), BF), VMEM((ROWS, HD), BF),
            VMEM((2, ROWS, HD), F32), VMEM((2, SHARDS, HD), F32), VMEM((8, SLOTS), jnp.int32),
            VMEM((ROWS, 6 * HD), BF), VMEM((2, ROWS, 2 * HD), BF), VMEM((2, ROWS, HD), BF),
            VMEM((SLOTS, 2 * HD), BF), VMEM((SLOTS, HD), BF), VMEM((ROWS, SLOTS), BF),
            VMEM((2 * ROWS, HD), BF), VMEM((2, CHIPS, CHIPS, BLK, HD), BF),
            VMEM((2 * ROWS, HD), F32), VMEM((2 * ROWS, 2 * HD), F32), VMEM((2 * ROWS, HD), BF),
            VMEM((8, 384, 512), BF), VMEM((4096, OUT), BF), VMEM((384, OUT), F32),
            dma((12,)), dma((SHARDS,)), dma((SHARDS,)), dma((SHARDS,)), dma((SHARDS,)),
            dma((4, GROUPS, CHIPS)), dma((GROUPS, CHIPS)), dma((GROUPS, CHIPS)),
            dma((8,)), dma((8,)), dma((8,)), dma((8,)),
            dma((CHIPS, 2)), dma((CHIPS, 2)), dma((3, 8)), dma((8,)),
        ],
        compiler_params=pltpu.CompilerParams(
            collective_id=0, has_side_effects=True, vmem_limit_bytes=56 << 20),
        cost_estimate=pl.CostEstimate(flops=13 * 10 ** 9, bytes_accessed=12 << 20, transcendentals=10 ** 7),
        name="layer",
    )(kept_count, keep_rank, query, key, value, *consts, out_weight)


def solution(mesh):
    placed = (P("ctx", "tp"), P("ctx", "tp"), P("ctx", "tp"), P("ctx", None), P(), P("tp", None))
    return jax.shard_map(
        local, mesh=mesh, in_specs=placed, out_specs=P("ctx", "tp"), check_vma=False)
```

```python
import math

import jax
import jax.numpy as jnp
import numpy as np
from jax import lax
from jax.experimental import pallas as pl
from jax.experimental.pallas import tpu as pltpu
from jax.sharding import PartitionSpec as P

HD = 128
ROWS = 768
BLK = 48
CHIPS = 16
SHARDS = 32
SLOTS = SHARDS * BLK
QL = 4
GROUPS = CHIPS // QL
LROWS = 2 * BLK
QROWS = QL * LROWS
STAGGER = 1
OUT = 1024
NT = (((1,), (1,)), ((), ()))
MESH = pl.DeviceIdType.MESH
VMEM = pltpu.VMEM
BF = jnp.bfloat16
F32 = jnp.float32


def tables():
    freq = 1000000.0 ** (-(np.arange(HD // 2) * 2.0 / HD))
    sign = np.concatenate([-np.ones(HD // 2), np.ones(HD // 2)])
    both = np.concatenate([freq, freq])
    own = np.arange(ROWS)[:, None] * both
    base = (np.arange(SHARDS) * ROWS)[:, None] * both
    col = np.arange(SLOTS)
    cols = np.zeros((8, SLOTS), np.int32)
    cols[0], cols[1] = col // BLK, col % BLK
    f = lambda a, b: np.stack([np.cos(a), np.sin(b) * sign]).astype(np.float32)
    return f(own, own), f(base, base), cols


def ctx_of(xl, z, core):
    return xl * 16 + z * 2 + core


def remote(src, dst, ssem, rsem, dev):
    return pltpu.make_async_remote_copy(
        src_ref=src, dst_ref=dst, send_sem=ssem, recv_sem=rsem, device_id=dev, device_id_type=MESH)


def at16(first, size):
    return pl.ds(pl.multiple_of(first, 16), size)


def layer_kernel(cnt, rank_h, q_h, k_h, v_h, own_h, base_h, cols_h, w_h, out,
                 rank, qin, kin, vin, own, base, cols,
                 xs, sq, skv, rq, rkv, unp, qs, kv, m_s, acc_s, o_s, af, wf, po,
                 ld, kv_s, kv_r, q_s, q_r, ring_s, ring_r, die_r, w_s, w_r, wd_s, wd_r,
                 a_s, a_r, g_s, g_r):
    c, t = lax.axis_index("ctx"), lax.axis_index("tp")
    core, z, xl, j, y, xh = c % 2, (c // 2) % 8, c // 16, c // 2, t // 2, t % 2
    mate = c + 1 - 2 * core
    bar = pltpu.get_barrier_semaphore()

    def landed(ref, sem):
        remote(ref, ref, sem, sem, (mate, t)).wait_recv()

    def left(ref, sem):
        remote(ref, ref, sem, sem, (mate, t)).wait_send()

    loads = {}
    wcol = pl.ds(pl.multiple_of(t * OUT, OUT), OUT)
    for n, (name, src, dst) in enumerate([
            ("rank", rank_h, rank), ("k", k_h, kin), ("own", own_h, own), ("base", base_h, base),
            ("v", v_h, vin), ("q", q_h, qin), ("cols", cols_h, cols),
            ("w", w_h.at[:, wcol], wf.at[pl.ds(pl.multiple_of(t * 512, 512), 512)])]):
        loads[name] = pltpu.make_async_copy(src, dst, ld.at[n])
        loads[name].start()

    def hail(i, _):
        pl.semaphore_signal(bar, inc=1, device_id=((c + i) % SHARDS, t), device_id_type=MESH)
        return 0
    lax.fori_loop(1, SHARDS, hail, 0)
    cx = ctx_of(1 - xl, z, core)
    w_peers = [(c, ((y + d) % 4) * 2 + xh) for d in (1, 2, 3)]
    w_peers += [(cx, ((y + d) % 4) * 2 + (1 - xh)) for d in (0, 1, 2, 3)]
    gat = [(c, y * 2 + 1 - xh), (c, ((y + 1) % 4) * 2 + xh), (c, ((y + 3) % 4) * 2 + xh)]
    for peer in w_peers + gat[:1]:
        pl.semaphore_signal(bar, inc=1, device_id=peer, device_id_type=MESH)

    loads["rank"].wait()
    my_count = cnt[c]
    start = jnp.int32(0)
    for s in range(SHARDS):
        start = start + jnp.where(s < c, cnt[s], 0)
    kept = rank[...] < my_count
    keptf = jnp.where(kept, 1.0, 0.0).astype(BF)
    i0 = lax.broadcasted_iota(jnp.int32, (ROWS, ROWS), 0)
    i1 = lax.broadcasted_iota(jnp.int32, (ROWS, ROWS), 1)
    tri = jnp.where(i0 < i1, 1.0, 0.0).astype(BF)
    order = jnp.dot(jnp.broadcast_to(keptf, (16, ROWS)), tri, preferred_element_type=F32)[0:1]
    slot = order.astype(jnp.int32) + lax.rem(start, jnp.int32(ROWS))
    slot = jnp.where(slot >= ROWS, slot - ROWS, slot)
    slot = jnp.where(kept, slot, -1)
    perm = jnp.where(i0 == slot, 1.0, 0.0).astype(BF)

    for name in ("own", "base", "k", "v"):
        loads[name].wait()
    cbr, sbr = base[0, pl.ds(c, 1), :], base[1, pl.ds(c, 1), :]
    civ, siv = own[0], own[1]
    cosv = civ * cbr - siv * sbr
    sinv = siv * cbr + civ * sbr

    def rotate(x, scale):
        x = x.astype(F32)
        r = x * cosv + pltpu.roll(x, HD // 2, 1) * sinv
        return (r * scale if scale else r).astype(BF)
    xs[:, 4 * HD:5 * HD] = rotate(kin[...], None)
    xs[:, 5 * HD:] = vin[...]
    kvp = jnp.dot(perm, xs[:, 4 * HD:], preferred_element_type=F32).astype(BF)
    skv[0] = kvp[:, :HD]
    skv[1] = kvp[:, HD:]
    pl.semaphore_wait(bar, SHARDS - 1 + 8)

    def kv_copy(d):
        return remote(skv.at[d % 2, at16((d // 2) * BLK, BLK)], rkv.at[at16(c * BLK, BLK)],
                      kv_s.at[0], kv_r.at[0], (d, t))

    def q_copy(d):
        return remote(sq.at[d % 2, at16((d // 2) * BLK, BLK)], rq.at[at16(c * BLK, BLK)],
                      q_s.at[0], q_r.at[0], (d, t))

    def start_kv(i, _):
        kv_copy((c + i) % SHARDS).start()
        return 0
    lax.fori_loop(1, SHARDS, start_kv, 0)
    own_kv = pltpu.make_async_copy(skv.at[core, at16(j * BLK, BLK)], rkv.at[at16(c * BLK, BLK)], ld.at[8])
    own_kv.start()

    half = 256

    def half_rows(b, cr):
        return wf.at[pl.ds(pl.multiple_of(b * 512 + cr * half, half), half)]

    def w_copy(n):
        peer = w_peers[n]
        return remote(w_h.at[pl.ds(pl.multiple_of(core * half, half), half),
                             pl.ds(pl.multiple_of(peer[1] * OUT, OUT), OUT)],
                      half_rows(t, core), w_s.at[0], w_r.at[t], peer)
    for n in range(7):
        w_copy(n).start()

    scale = math.log2(math.e) / math.sqrt(HD)
    loads["q"].wait()
    for h in range(4):
        xs[:, h * HD:(h + 1) * HD] = rotate(qin[:, h * HD:(h + 1) * HD], scale)
    qp = jnp.dot(perm, xs[:, :4 * HD], preferred_element_type=F32).astype(BF)
    sq[0] = qp[:, :2 * HD]
    sq[1] = qp[:, 2 * HD:]

    def start_q(i, _):
        q_copy((c + i) % SHARDS).start()
        return 0
    lax.fori_loop(1, SHARDS, start_q, 0)
    own_q = pltpu.make_async_copy(sq.at[core, at16(j * BLK, BLK)], rq.at[at16(c * BLK, BLK)], ld.at[9])
    own_q.start()

    loads["cols"].wait()
    grp, mod = cols[0:1, :], cols[1:2, :]
    first = jnp.zeros((1, SLOTS), jnp.int32)
    last = jnp.zeros((1, SLOTS), jnp.int32)
    for s in range(SHARDS):
        first = first + jnp.where(grp > s, cnt[s], 0)
        last = last + jnp.where(grp >= s, cnt[s], 0)
    isub = lax.broadcasted_iota(jnp.int32, (BLK, SLOTS), 0)
    for lv in range(CHIPS):
        num = mod + (lv * ROWS + j * BLK)
        sel = jnp.where((first <= num) & (num < last), mod, -1)
        unp[lv * BLK:(lv + 1) * BLK, :] = jnp.where(isub == sel, 1.0, 0.0).astype(BF)
    m_s[...] = jnp.full(m_s.shape, -1e30, F32)
    acc_s[...] = jnp.zeros(acc_s.shape, F32)

    own_kv.wait()

    rest = (SHARDS - 1) * BLK
    landed(rkv.at[pl.ds(0, rest)], kv_r.at[0])
    mine = jnp.dot(unp[...], rkv[...], preferred_element_type=F32).astype(BF)
    kv[core, j] = mine.reshape(CHIPS, BLK, HD)

    count = [0] * 4
    ways = [(ctx_of(xl, (z + 1) % 8, core), t), (ctx_of(xl, (z + 7) % 8, core), t), (cx, t), (mate, t)]
    RIGHT, LEFT, CROSS, DIE = range(4)

    def piece(g, b):
        return kv.at[core, b, pl.ds(g * QL, QL)]

    def go(g, b, *to):
        for way in to:
            rsem = die_r.at[g] if way == DIE else ring_r.at[g, b]
            remote(piece(g, b), piece(g, b), ring_s.at[way], rsem, ways[way]).start()
            count[way] += 1

    def arrive(g, b, *to):
        landed(piece(g, b), ring_r.at[g, b])
        go(g, b, *to)

    def same(d):
        return xl * 8 + (z + 8 + d) % 8

    def other(d):
        return (1 - xl) * 8 + (z + 8 + d) % 8

    routes = [(3, 4, 2, 1), (4, 3, 0, 1)]

    def tick(g, k):
        own_r, own_l, far_r, far_l = routes[g % 2]
        if k == 0:
            go(g, j, RIGHT, LEFT, CROSS, DIE)
        if k == 1:
            arrive(g, other(0), *([RIGHT] * (far_r > 0) + [LEFT] * (far_l > 0) + [DIE]))
        for d, way, hops, far in ((-k, RIGHT, own_r, far_r), (k, LEFT, own_l, far_l)):
            if 1 <= k <= hops:
                arrive(g, same(d), *([way] * (k < hops) + [CROSS] * (k > far) + [DIE]))
        for d, way, hops, far in ((1 - k, RIGHT, own_r, far_r), (k - 1, LEFT, own_l, far_l)):
            if 1 <= k - 1 <= hops:
                arrive(g, other(d), *([way] * (k - 1 < far) + [DIE]))

    def whole(g):
        landed(kv.at[1 - core, :, pl.ds(g * QL, QL)], die_r.at[g])

    def update(r0, n, s, vals):
        rows = pl.ds(r0, n)
        mo = m_s[rows, :]
        mn = jnp.maximum(mo, jnp.max(s, axis=1, keepdims=True))
        a = jnp.exp2(mo - mn)
        p = jnp.exp2(s - jnp.tile(mn, (1, s.shape[1] // HD))).astype(BF)
        m_s[rows, :] = mn
        vo = jnp.concatenate([vals, jnp.ones(vals.shape, BF)], axis=1)
        acc_s[rows, :] = acc_s[rows, :] * jnp.tile(a, (1, 2)) + jnp.dot(p, vo, preferred_element_type=F32)

    def unit(g, b):
        r0 = b * QROWS
        if b > g:
            n = QROWS // 2
            lv = slice(g * QL, (g + 1) * QL)
            kk = kv[0, :, lv].reshape(QL * ROWS, HD)
            vv = kv[1, :, lv].reshape(QL * ROWS, HD)
            ss = [lax.dot_general(qs[r0 + h * n:r0 + (h + 1) * n, :], kk, NT, preferred_element_type=F32)
                  for h in range(2)]
            for h in range(2):
                update(r0 + h * n, n, ss[h], vv)
            return
        for i in range(QL):
            lv = g * QL + i
            rs, n = r0 + i * LROWS, QROWS - i * LROWS
            kk = kv[0, :, lv].reshape(ROWS, HD)
            vv = kv[1, :, lv].reshape(ROWS, HD)
            s = lax.dot_general(qs[rs:rs + n, :], kk, NT, preferred_element_type=F32)
            r = lax.broadcasted_iota(jnp.int32, (LROWS, ROWS), 0)
            lim = jnp.where(r >= BLK, r - BLK, r) + j * BLK
            col = lax.broadcasted_iota(jnp.int32, (LROWS, ROWS), 1)
            top = jnp.where(col <= lim, s[:LROWS], -1e30)
            s = top if n == LROWS else jnp.concatenate([top, s[LROWS:]], axis=0)
            update(rs, n, s, vv)

    def here(h):
        return af.at[t, at16(z * BLK, BLK), pl.ds(pl.multiple_of(core * 256 + h * HD, HD), HD)]

    def o_copy(lv, h):
        return remote(o_s.at[pl.ds(lv * LROWS + h * BLK, BLK)], here(h), a_s.at[0], a_r.at[0],
                      (2 * lv + xl, t))

    def o_own(lv, h):
        return pltpu.make_async_copy(o_s.at[pl.ds(lv * LROWS + h * BLK, BLK)], here(h), ld.at[10 + h])

    def finish(b):
        rows = pl.ds(b * QROWS, QROWS)
        o_s[rows, :] = (acc_s[rows, :HD] / acc_s[rows, HD:]).astype(BF)
        for lv in range(b * QL, (b + 1) * QL):
            @pl.when(2 * lv + xl != c)
            def _():
                o_copy(lv, 0).start()
                o_copy(lv, 1).start()

            @pl.when(2 * lv + xl == c)
            def _():
                o_own(lv, 0).start()
                o_own(lv, 1).start()

    def take_queries():
        own_q.wait()
        landed(rq.at[pl.ds(0, rest)], q_r.at[0])
        r = jnp.dot(unp[...], rq[...], preferred_element_type=F32).astype(BF)
        for lv in range(CHIPS):
            for h in range(2):
                qs[lv * LROWS + h * BLK:lv * LROWS + (h + 1) * BLK, :] = r[
                    lv * BLK:(lv + 1) * BLK, h * HD:(h + 1) * HD]

    work = {g: [(g, b) for b in range(g, GROUPS)] for g in range(GROUPS)}
    ready, todo = 0, []
    for step in range(STAGGER * (GROUPS - 1) + 6):
        for g in range(GROUPS):
            if 0 <= step - STAGGER * g <= 5:
                tick(g, step - STAGGER * g)
        if step == 4:
            take_queries()
        if step - STAGGER * ready == 5:
            whole(ready)
            todo += work[ready]
            ready += 1
        for _ in range(2 if ready < GROUPS else len(todo)):
            if todo:
                g, b = todo.pop(0)
                unit(g, b)
                if g == b:
                    finish(b)

    for n in range(7):
        b = w_peers[n][1]
        landed(half_rows(b, core), w_r.at[b])
        remote(half_rows(b, core), half_rows(b, core), wd_s.at[0], wd_r.at[b], (mate, t)).start()
    loads["w"].wait()

    mixed = xl == core

    @pl.when(mixed)
    def _():
        o_own(0, 0).wait()
        o_own(0, 1).wait()
        landed(o_s.at[pl.ds(0, 15 * LROWS)], a_r.at[0])

    @pl.when(jnp.logical_not(mixed))
    def _():
        landed(o_s, a_r.at[0])

    def pass_on(b, *to):
        for way in to:
            remote(af.at[b], af.at[b], g_s.at[0], g_r.at[b], gat[way]).start()

    def got(b, *to):
        landed(af.at[b], g_r.at[b])
        pass_on(b, *to)

    def mul(b, begin=False):
        rows = pl.ds(pl.multiple_of(b * 512, 512), 512)
        if not begin:
            landed(half_rows(b, 1 - core), wd_r.at[b])

        @pl.loop(0, OUT // 256)
        def _(n):
            cs = pl.ds(pl.multiple_of(n * 256, 256), 256)
            part = jnp.dot(af[b], wf[rows, cs], preferred_element_type=F32)
            po[:, cs] = part if begin else po[:, cs] + part

    lo, hi, opp = (y + 3) % 4, (y + 1) % 4, (y + 2) % 4
    pass_on(t, 0, 1, 2)
    mul(t, True)
    bx = y * 2 + 1 - xh
    got(bx, 1, 2)
    got(lo * 2 + xh, 1)
    mul(bx)
    mul(lo * 2 + xh)
    got(hi * 2 + xh)
    mul(hi * 2 + xh)
    got(hi * 2 + 1 - xh, 2)
    mul(hi * 2 + 1 - xh)
    got(lo * 2 + 1 - xh)
    mul(lo * 2 + 1 - xh)
    got(opp * 2 + xh)
    mul(opp * 2 + xh)
    got(opp * 2 + 1 - xh)
    mul(opp * 2 + 1 - xh)
    out[...] = po[...].astype(BF)

    left(af.at[pl.ds(0, 7)], g_s.at[0])
    left(wf.at[pl.ds(0, 7 * half)], w_s.at[0])
    left(wf.at[pl.ds(0, 7 * half)], wd_s.at[0])
    for way in range(4):
        parts = 1 if count[way] % 4 == 0 else 2
        left(kv.at[0, pl.ds(0, parts * count[way] // 4), pl.ds(0, CHIPS // parts)], ring_s.at[way])

    @pl.when(mixed)
    def _():
        left(o_s.at[pl.ds(0, 15 * LROWS)], a_s.at[0])

    @pl.when(jnp.logical_not(mixed))
    def _():
        left(o_s, a_s.at[0])
    left(rkv.at[pl.ds(0, rest)], kv_s.at[0])
    left(rq.at[pl.ds(0, rest)], q_s.at[0])


def local(query, key, value, keep_rank, kept_count, out_weight):
    dma = pltpu.SemaphoreType.DMA
    consts = [jnp.asarray(a) for a in tables()]
    hbm = pl.BlockSpec(memory_space=pl.ANY)
    return pl.pallas_call(
        layer_kernel,
        out_shape=jax.ShapeDtypeStruct((384, OUT), BF),
        in_specs=[pl.BlockSpec(memory_space=pltpu.SMEM)] + [hbm] * 8,
        out_specs=pl.BlockSpec(memory_space=VMEM),
        scratch_shapes=[
            VMEM((1, ROWS), jnp.int32), VMEM((ROWS, 4 * HD), BF), VMEM((ROWS, HD), BF), VMEM((ROWS, HD), BF),
            VMEM((2, ROWS, HD), F32), VMEM((2, SHARDS, HD), F32), VMEM((8, SLOTS), jnp.int32),
            VMEM((ROWS, 6 * HD), BF), VMEM((2, ROWS, 2 * HD), BF), VMEM((2, ROWS, HD), BF),
            VMEM((SLOTS, 2 * HD), BF), VMEM((SLOTS, HD), BF), VMEM((ROWS, SLOTS), BF),
            VMEM((2 * ROWS, HD), BF), VMEM((2, CHIPS, CHIPS, BLK, HD), BF),
            VMEM((2 * ROWS, HD), F32), VMEM((2 * ROWS, 2 * HD), F32), VMEM((2 * ROWS, HD), BF),
            VMEM((8, 384, 512), BF), VMEM((4096, OUT), BF), VMEM((384, OUT), F32),
            dma((12,)), dma((1,)), dma((1,)), dma((1,)), dma((1,)),
            dma((4,)), dma((GROUPS, CHIPS)), dma((GROUPS,)),
            dma((1,)), dma((8,)), dma((1,)), dma((8,)),
            dma((1,)), dma((1,)), dma((1,)), dma((8,)),
        ],
        compiler_params=pltpu.CompilerParams(
            collective_id=0, has_side_effects=True, vmem_limit_bytes=56 << 20),
        cost_estimate=pl.CostEstimate(flops=13 * 10 ** 9, bytes_accessed=12 << 20, transcendentals=10 ** 7),
        name="layer",
    )(kept_count, keep_rank, query, key, value, *consts, out_weight)


def solution(mesh):
    placed = (P("ctx", "tp"), P("ctx", "tp"), P("ctx", "tp"), P("ctx", None), P(), P("tp", None))
    return jax.shard_map(
        local, mesh=mesh, in_specs=placed, out_specs=P("ctx", "tp"), check_vma=False)
```

```python
import math

import jax
import jax.numpy as jnp
import numpy as np
from jax import lax
from jax.experimental import pallas as pl
from jax.experimental.pallas import tpu as pltpu
from jax.sharding import PartitionSpec as P

HD = 128
ROWS = 768
BLK = 48
CHIPS = 16
SHARDS = 32
SLOTS = SHARDS * BLK
QL = 4
GROUPS = CHIPS // QL
QROWS = QL * BLK
SECOND = 6
OUT = 1024
NT = (((1,), (1,)), ((), ()))
MESH = pl.DeviceIdType.MESH
VMEM = pltpu.VMEM
BF = jnp.bfloat16
F32 = jnp.float32


def tables():
    freq = 1000000.0 ** (-(np.arange(HD // 2) * 2.0 / HD))
    sign = np.concatenate([-np.ones(HD // 2), np.ones(HD // 2)])
    both = np.concatenate([freq, freq])
    own = np.arange(ROWS)[:, None] * both
    base = (np.arange(SHARDS) * ROWS)[:, None] * both
    col = np.arange(SLOTS)
    cols = np.zeros((8, SLOTS), np.int32)
    cols[0], cols[1] = col // BLK, col % BLK
    f = lambda a, b: np.stack([np.cos(a), np.sin(b) * sign]).astype(np.float32)
    return f(own, own), f(base, base), cols


def ctx_of(xl, z, core):
    return xl * 16 + z * 2 + core


def remote(src, dst, ssem, rsem, dev):
    return pltpu.make_async_remote_copy(
        src_ref=src, dst_ref=dst, send_sem=ssem, recv_sem=rsem, device_id=dev, device_id_type=MESH)


def at16(first, size):
    return pl.ds(pl.multiple_of(first, 16), size)


def layer_kernel(cnt, rank_h, q_h, k_h, v_h, own_h, base_h, cols_h, w_h, out,
                 rank, qin, kin, vin, own, base, cols,
                 xs, sq, skv, rq, rkv, unp, qs, kv, m_s, acc_s, o_s, af, wf, po,
                 ld, kv_s, kv_r, q_s, q_r, ring_s, ring_r, die_r, w_s, w_r, wd_s, wd_r,
                 a_s, a_r, g_s, g_r):
    c, t = lax.axis_index("ctx"), lax.axis_index("tp")
    core, z, xl, j, y, xh = c % 2, (c // 2) % 8, c // 16, c // 2, t // 2, t % 2
    mate = c + 1 - 2 * core
    bar = pltpu.get_barrier_semaphore()

    def landed(ref, sem):
        remote(ref, ref, sem, sem, (mate, t)).wait_recv()

    def left(ref, sem):
        remote(ref, ref, sem, sem, (mate, t)).wait_send()

    loads = {}
    wcol = pl.ds(pl.multiple_of(t * OUT, OUT), OUT)
    for n, (name, src, dst) in enumerate([
            ("rank", rank_h, rank), ("k", k_h, kin), ("own", own_h, own), ("base", base_h, base),
            ("v", v_h, vin), ("q", q_h, qin), ("cols", cols_h, cols),
            *[(f"w{n}", w_h.at[pl.ds(n * 128, 128), wcol],
               wf.at[n % 2, pl.ds(pl.multiple_of(t * 256 + n // 2 * 128, 128), 128)]) for n in range(4)]]):
        loads[name] = pltpu.make_async_copy(src, dst, ld.at[n])
        loads[name].start()

    def hail(i, _):
        pl.semaphore_signal(bar, inc=1, device_id=((c + i) % SHARDS, t), device_id_type=MESH)
        return 0
    lax.fori_loop(1, SHARDS, hail, 0)
    cx = ctx_of(1 - xl, z, core)
    w_peers = [(c, ((y + d) % 4) * 2 + xh) for d in (1, 2, 3)]
    w_peers += [(cx, ((y + d) % 4) * 2 + (1 - xh)) for d in (0, 1, 2, 3)]
    gat = [(c, y * 2 + 1 - xh), (c, ((y + 1) % 4) * 2 + xh), (c, ((y + 3) % 4) * 2 + xh)]
    for peer in w_peers + gat[:1]:
        pl.semaphore_signal(bar, inc=1, device_id=peer, device_id_type=MESH)

    loads["rank"].wait()
    my_count = cnt[c]
    start = jnp.int32(0)
    for s in range(SHARDS):
        start = start + jnp.where(s < c, cnt[s], 0)
    kept = rank[...] < my_count
    keptf = jnp.where(kept, 1.0, 0.0).astype(BF)
    i0 = lax.broadcasted_iota(jnp.int32, (ROWS, ROWS), 0)
    i1 = lax.broadcasted_iota(jnp.int32, (ROWS, ROWS), 1)
    tri = jnp.where(i0 < i1, 1.0, 0.0).astype(BF)
    order = jnp.dot(jnp.broadcast_to(keptf, (16, ROWS)), tri, preferred_element_type=F32)[0:1]
    slot = order.astype(jnp.int32) + lax.rem(start, jnp.int32(ROWS))
    slot = jnp.where(slot >= ROWS, slot - ROWS, slot)
    slot = jnp.where(kept, slot, -1)
    perm = jnp.where(i0 == slot, 1.0, 0.0).astype(BF)

    for name in ("own", "base", "k", "v"):
        loads[name].wait()
    cbr, sbr = base[0, pl.ds(c, 1), :], base[1, pl.ds(c, 1), :]
    civ, siv = own[0], own[1]
    cosv = civ * cbr - siv * sbr
    sinv = siv * cbr + civ * sbr

    def rotate(x, scale):
        x = x.astype(F32)
        r = x * cosv + pltpu.roll(x, HD // 2, 1) * sinv
        return (r * scale if scale else r).astype(BF)
    xs[:, 4 * HD:5 * HD] = rotate(kin[...], None)
    xs[:, 5 * HD:] = vin[...]
    kvp = jnp.dot(perm, xs[:, 4 * HD:], preferred_element_type=F32).astype(BF)
    skv[0] = kvp[:, :HD]
    skv[1] = kvp[:, HD:]
    pl.semaphore_wait(bar, SHARDS - 1 + 8)

    def kv_copy(d):
        return remote(skv.at[d % 2, at16((d // 2) * BLK, BLK)], rkv.at[at16(c * BLK, BLK)],
                      kv_s.at[0], kv_r.at[0], (d, t))

    def q_copy(d, h):
        return remote(sq.at[2 * (d % 2) + h, at16((d // 2) * BLK, BLK)], rq.at[h, at16(c * BLK, BLK)],
                      q_s.at[h], q_r.at[h], (d, t))

    def start_kv(i, _):
        kv_copy((c + i) % SHARDS).start()
        return 0
    lax.fori_loop(1, SHARDS, start_kv, 0)
    own_kv = pltpu.make_async_copy(skv.at[core, at16(j * BLK, BLK)], rkv.at[at16(c * BLK, BLK)], ld.at[11])
    own_kv.start()

    def half_rows(h, b, cr):
        return wf.at[h, pl.ds(pl.multiple_of(b * 256 + cr * 128, 128), 128)]

    def w_copy(n, h):
        peer = w_peers[n]
        return remote(w_h.at[pl.ds(pl.multiple_of(core * 256 + h * 128, 128), 128),
                             pl.ds(pl.multiple_of(peer[1] * OUT, OUT), OUT)],
                      half_rows(h, t, core), w_s.at[0], w_r.at[t], peer)
    for n in range(7):
        w_copy(n, 0).start()
        w_copy(n, 1).start()

    scale = math.log2(math.e) / math.sqrt(HD)
    loads["q"].wait()
    for h in range(4):
        xs[:, h * HD:(h + 1) * HD] = rotate(qin[:, h * HD:(h + 1) * HD], scale)
    qp = jnp.dot(perm, xs[:, :4 * HD], preferred_element_type=F32).astype(BF)
    for h in range(4):
        sq[h] = qp[:, h * HD:(h + 1) * HD]

    def send_queries(h):
        def start_q(i, _):
            q_copy((c + i) % SHARDS, h).start()
            return 0
        lax.fori_loop(1, SHARDS, start_q, 0)
    own_q = [pltpu.make_async_copy(sq.at[2 * core + h, at16(j * BLK, BLK)], rq.at[h, at16(c * BLK, BLK)],
                                   ld.at[12 + h]) for h in range(2)]
    own_q[0].start()
    own_q[1].start()
    send_queries(0)

    loads["cols"].wait()
    grp, mod = cols[0:1, :], cols[1:2, :]
    first = jnp.zeros((1, SLOTS), jnp.int32)
    last = jnp.zeros((1, SLOTS), jnp.int32)
    for s in range(SHARDS):
        first = first + jnp.where(grp > s, cnt[s], 0)
        last = last + jnp.where(grp >= s, cnt[s], 0)
    isub = lax.broadcasted_iota(jnp.int32, (BLK, SLOTS), 0)
    for lv in range(CHIPS):
        num = mod + (lv * ROWS + j * BLK)
        sel = jnp.where((first <= num) & (num < last), mod, -1)
        unp[lv * BLK:(lv + 1) * BLK, :] = jnp.where(isub == sel, 1.0, 0.0).astype(BF)
    m_s[...] = jnp.full(m_s.shape, -1e30, F32)
    acc_s[...] = jnp.zeros(acc_s.shape, F32)

    own_kv.wait()

    rest = (SHARDS - 1) * BLK
    landed(rkv.at[pl.ds(0, rest)], kv_r.at[0])
    mine = jnp.dot(unp[...], rkv[...], preferred_element_type=F32).astype(BF)
    kv[core, j] = mine.reshape(CHIPS, BLK, HD)

    count = [0] * 4
    ways = [(ctx_of(xl, (z + 1) % 8, core), t), (ctx_of(xl, (z + 7) % 8, core), t), (cx, t), (mate, t)]
    RIGHT, LEFT, CROSS, DIE = range(4)

    def piece(g, b):
        return kv.at[core, b, pl.ds(g * QL, QL)]

    def go(g, b, *to):
        for way in to:
            rsem = die_r.at[g] if way == DIE else ring_r.at[g, b]
            remote(piece(g, b), piece(g, b), ring_s.at[way], rsem, ways[way]).start()
            count[way] += 1

    def arrive(g, b, *to):
        landed(piece(g, b), ring_r.at[g, b])
        go(g, b, *to)

    def same(d):
        return xl * 8 + (z + 8 + d) % 8

    def other(d):
        return (1 - xl) * 8 + (z + 8 + d) % 8

    routes = [(3, 4, 2, 1), (4, 3, 0, 1)]

    def tick(g, k):
        own_r, own_l, far_r, far_l = routes[g % 2]
        if k == 0:
            go(g, j, RIGHT, LEFT, CROSS, DIE)
        if k == 1:
            arrive(g, other(0), *([RIGHT] * (far_r > 0) + [LEFT] * (far_l > 0) + [DIE]))
        for d, way, hops, far in ((-k, RIGHT, own_r, far_r), (k, LEFT, own_l, far_l)):
            if 1 <= k <= hops:
                arrive(g, same(d), *([way] * (k < hops) + [CROSS] * (k > far) + [DIE]))
        for d, way, hops, far in ((1 - k, RIGHT, own_r, far_r), (k - 1, LEFT, own_l, far_l)):
            if 1 <= k - 1 <= hops:
                arrive(g, other(d), *([way] * (k - 1 < far) + [DIE]))

    def whole(g):
        landed(kv.at[1 - core, :, pl.ds(g * QL, QL)], die_r.at[g])

    def update(r0, n, s, vals):
        rows = pl.ds(r0, n)
        mo = m_s[rows, :]
        mn = jnp.maximum(mo, jnp.max(s, axis=1, keepdims=True))
        a = jnp.exp2(mo - mn)
        p = jnp.exp2(s - jnp.tile(mn, (1, s.shape[1] // HD))).astype(BF)
        m_s[rows, :] = mn
        vo = jnp.concatenate([vals, jnp.ones(vals.shape, BF)], axis=1)
        acc_s[rows, :] = acc_s[rows, :] * jnp.tile(a, (1, 2)) + jnp.dot(p, vo, preferred_element_type=F32)

    def unit(g, h):
        lv = slice(g * QL, (g + 1) * QL)
        kk = kv[0, :, lv].reshape(QL * ROWS, HD)
        vv = kv[1, :, lv].reshape(QL * ROWS, HD)
        later = range(g + 1, GROUPS)
        ss = [lax.dot_general(qs[h, b * QROWS:(b + 1) * QROWS, :], kk, NT, preferred_element_type=F32)
              for b in later]
        for b, s in zip(later, ss):
            update(h * ROWS + b * QROWS, QROWS, s, vv)
        for i in range(QL):
            lv = g * QL + i
            rs, n = lv * BLK, QROWS - i * BLK
            kk = kv[0, :, lv].reshape(ROWS, HD)
            vv = kv[1, :, lv].reshape(ROWS, HD)
            s = lax.dot_general(qs[h, rs:rs + n, :], kk, NT, preferred_element_type=F32)
            lim = lax.broadcasted_iota(jnp.int32, (BLK, ROWS), 0) + j * BLK
            col = lax.broadcasted_iota(jnp.int32, (BLK, ROWS), 1)
            top = jnp.where(col <= lim, s[:BLK], -1e30)
            s = top if n == BLK else jnp.concatenate([top, s[BLK:]], axis=0)
            update(h * ROWS + rs, n, s, vv)
        finish(g, h)

    def here(h):
        return af.at[h, t, at16(z * BLK, BLK), pl.ds(pl.multiple_of(core * HD, HD), HD)]

    def o_copy(lv, h):
        return remote(o_s.at[h, pl.ds(lv * BLK, BLK)], here(h), a_s.at[h], a_r.at[h], (2 * lv + xl, t))

    def o_own(lv, h):
        return pltpu.make_async_copy(o_s.at[h, pl.ds(lv * BLK, BLK)], here(h), ld.at[14 + h])

    def finish(b, h):
        rows = pl.ds(h * ROWS + b * QROWS, QROWS)
        o_s[h, pl.ds(b * QROWS, QROWS), :] = (acc_s[rows, :HD] / acc_s[rows, HD:]).astype(BF)
        for lv in range(b * QL, (b + 1) * QL):
            @pl.when(2 * lv + xl != c)
            def _():
                o_copy(lv, h).start()

            @pl.when(2 * lv + xl == c)
            def _():
                o_own(lv, h).start()

    mixed = xl == core

    def take_rows(h):
        @pl.when(mixed)
        def _():
            o_own(0, h).wait()
            landed(o_s.at[h, pl.ds(0, 15 * BLK)], a_r.at[h])

        @pl.when(jnp.logical_not(mixed))
        def _():
            landed(o_s.at[h], a_r.at[h])

    def take_queries(h):
        own_q[h].wait()
        landed(rq.at[h, pl.ds(0, rest)], q_r.at[h])
        qs[h] = jnp.dot(unp[...], rq[h], preferred_element_type=F32).astype(BF)

    for step in range(GROUPS + 5):
        for g in range(GROUPS):
            if 0 <= step - g <= 5:
                tick(g, step - g)
        if step == SECOND:
            send_queries(1)
        if step == 4:
            take_queries(0)
        if step >= 5:
            whole(step - 5)
            unit(step - 5, 0)

    def pass_on(h, b, *to):
        for way in to:
            remote(af.at[h, b], af.at[h, b], g_s.at[0], g_r.at[h, b], gat[way]).start()

    def got(h, b, *to):
        landed(af.at[h, b], g_r.at[h, b])
        pass_on(h, b, *to)

    def mul(h, b, begin=False):
        rows = pl.ds(pl.multiple_of(b * 256, 256), 256)
        if h == 0 and not begin:
            landed(wf.at[0, pl.ds(0, 256)], wd_r.at[b])

        @pl.loop(0, OUT // 256)
        def _(n):
            cs = pl.ds(pl.multiple_of(n * 256, 256), 256)
            part = jnp.dot(af[h, b], wf[h, rows, cs], preferred_element_type=F32)
            po[:, cs] = part if begin else po[:, cs] + part

    lo, hi, opp = (y + 3) % 4 * 2, (y + 1) % 4 * 2, (y + 2) % 4 * 2
    bx, nx = y * 2 + 1 - xh, 1 - xh
    take_rows(0)
    pass_on(0, t, 0, 1, 2)
    take_queries(1)
    unit(0, 1)
    got(0, bx, 1, 2)
    got(0, lo + xh, 1)
    unit(1, 1)
    got(0, hi + xh)
    got(0, hi + nx, 2)
    unit(2, 1)
    unit(3, 1)
    for n in range(7):
        b = w_peers[n][1]
        landed(wf.at[0, pl.ds(0, 256)], w_r.at[b])
        for h in range(2):
            remote(half_rows(h, b, core), half_rows(h, b, core), wd_s.at[0], wd_r.at[b], (mate, t)).start()
    for n in range(4):
        loads[f"w{n}"].wait()

    mul(0, t, True)
    mul(0, bx)
    mul(0, lo + xh)
    take_rows(1)
    pass_on(1, t, 0, 1, 2)
    mul(0, hi + xh)
    mul(0, hi + nx)
    for b in (lo + nx, opp + xh, opp + nx):
        got(0, b)
        mul(0, b)
    mul(1, t)
    got(1, bx, 1, 2)
    got(1, lo + xh, 1)
    mul(1, bx)
    mul(1, lo + xh)
    got(1, hi + nx, 2)
    mul(1, hi + nx)
    for b in (hi + xh, lo + nx, opp + xh, opp + nx):
        got(1, b)
        mul(1, b)
    out[...] = po[...].astype(BF)

    left(af.at[:, pl.ds(0, 7)], g_s.at[0])
    left(wf.at[0, pl.ds(0, 7 * 256)], w_s.at[0])
    left(wf.at[0, pl.ds(0, 7 * 256)], wd_s.at[0])
    for way in range(4):
        parts = 1 if count[way] % 4 == 0 else 2
        left(kv.at[0, pl.ds(0, parts * count[way] // 4), pl.ds(0, CHIPS // parts)], ring_s.at[way])
    for h in range(2):
        left(rq.at[h, pl.ds(0, rest)], q_s.at[h])

        @pl.when(mixed)
        def _():
            left(o_s.at[h, pl.ds(0, 15 * BLK)], a_s.at[h])

        @pl.when(jnp.logical_not(mixed))
        def _():
            left(o_s.at[h], a_s.at[h])
    left(rkv.at[pl.ds(0, rest)], kv_s.at[0])


def local(query, key, value, keep_rank, kept_count, out_weight):
    dma = pltpu.SemaphoreType.DMA
    consts = [jnp.asarray(a) for a in tables()]
    hbm = pl.BlockSpec(memory_space=pl.ANY)
    return pl.pallas_call(
        layer_kernel,
        out_shape=jax.ShapeDtypeStruct((384, OUT), BF),
        in_specs=[pl.BlockSpec(memory_space=pltpu.SMEM)] + [hbm] * 8,
        out_specs=pl.BlockSpec(memory_space=VMEM),
        scratch_shapes=[
            VMEM((1, ROWS), jnp.int32), VMEM((ROWS, 4 * HD), BF), VMEM((ROWS, HD), BF), VMEM((ROWS, HD), BF),
            VMEM((2, ROWS, HD), F32), VMEM((2, SHARDS, HD), F32), VMEM((8, SLOTS), jnp.int32),
            VMEM((ROWS, 6 * HD), BF), VMEM((4, ROWS, HD), BF), VMEM((2, ROWS, HD), BF),
            VMEM((2, SLOTS, HD), BF), VMEM((SLOTS, HD), BF), VMEM((ROWS, SLOTS), BF),
            VMEM((2, ROWS, HD), BF), VMEM((2, CHIPS, CHIPS, BLK, HD), BF),
            VMEM((2 * ROWS, HD), F32), VMEM((2 * ROWS, 2 * HD), F32), VMEM((2, ROWS, HD), BF),
            VMEM((2, 8, 384, 256), BF), VMEM((2, 2048, OUT), BF), VMEM((384, OUT), F32),
            dma((16,)), dma((1,)), dma((1,)), dma((2,)), dma((2,)),
            dma((4,)), dma((GROUPS, CHIPS)), dma((GROUPS,)),
            dma((1,)), dma((8,)), dma((1,)), dma((8,)),
            dma((2,)), dma((2,)), dma((1,)), dma((2, 8)),
        ],
        compiler_params=pltpu.CompilerParams(
            collective_id=0, has_side_effects=True, vmem_limit_bytes=56 << 20),
        cost_estimate=pl.CostEstimate(flops=13 * 10 ** 9, bytes_accessed=12 << 20, transcendentals=10 ** 7),
        name="layer",
    )(kept_count, keep_rank, query, key, value, *consts, out_weight)


def solution(mesh):
    placed = (P("ctx", "tp"), P("ctx", "tp"), P("ctx", "tp"), P("ctx", None), P(), P("tp", None))
    return jax.shard_map(
        local, mesh=mesh, in_specs=placed, out_specs=P("ctx", "tp"), check_vma=False)
```
